32 devices in a mesh: seq: 16 (over z, y, core), head: 2 (over x).
Axes of the slice: x: 2, y: 2, z: 4, core: 2. Of those that a mesh axis runs over, the one named last changes fastest.
Arguments:
- inputs: bfloat16 [8192, 5376], P('seq'), may hold values from -6 to 6
- queries: bfloat16 [8192, 4096], P('seq', 'head'), may hold values from -6 to 6
- key_matrix: bfloat16 [5376, 2048], P('seq', 'head'), may hold values from -0.078125 to 0.078125
- value_matrix: bfloat16 [5376, 2048], P('seq', 'head'), may hold values from -0.078125 to 0.078125
- readout: bfloat16 [4096, 512], P('head'), may hold values from -6 to 6
- token_mask: int32 [8192], P('seq'), may hold values 0 or 1
- targets: int32 [8192], P('seq'), may hold values from 0 to 511
Outputs:
- query_grad: float32 [8192, 4096], P('seq', 'head')
- input_grad: float32 [8192, 5376], P('seq', 'head')
The draws below stay inside these ranges and needn't reach their ends.
All inputs are finite; a program needn't handle non-finite values. No bound on the sum of `token_mask` on one device may be relied on, other than what follows from the above.
Results may differ from the reference program's by a relative error of at most 0.028.
Values may be sent and summed in bfloat16 or wider, within the bound.
A program may use at most 256 MiB of HBM per device.

```python
import jax
import jax.numpy as jnp
from jax import lax

MODEL_WIDTH = 5376
QUERY_HEADS = 32
KEY_VALUE_HEADS = 16
HEAD_SIZE = 128
WINDOW_KEYS = 1024
LOCAL_TOKENS = 512
CAND = 512
SEQUENCE_TOKENS = 8192
N_HEAD = 2


def plant(array, rng, low, high):
    longest = array.shape.index(max(array.shape))
    spots = []
    for shift in (0, 1):
        where = [jax.random.randint(jax.random.fold_in(rng, axis), (), 0, length) for axis, length in enumerate(array.shape)]
        where[longest] = (where[longest] + shift) % array.shape[longest]
        spots.append(tuple(where))
    return array.at[spots[0]].set(low).at[spots[1]].set(high)


def level_of(rng, extent, cuts, smallest, top_value):
    gain = 1.0
    for position, shards_of in cuts:
        heights = jax.random.uniform(jax.random.fold_in(jax.random.fold_in(rng, 6), position), (shards_of,), jnp.float32, smallest / len(cuts), top_value / len(cuts))
        gain = gain * jnp.repeat(jnp.exp(heights), extent[position] // shards_of).reshape((-1,) + (1,) * (len(extent) - 1 - position))
    return gain


def scatter_about(own_key, dims, scale, limit, cuts=(), kind=jnp.bfloat16):
    result = jax.random.normal(own_key, dims, jnp.float32) * scale
    if len(cuts) > 0:
        result = level_of(own_key, dims, cuts, -0.22, 0.18) * result
    return jnp.clip(result, min=-limit, max=limit).astype(kind)


def setup_inputs(seed: int = 0) -> dict:
    streams_of = jax.random.split(jax.random.key(seed), 8)
    return {
        "inputs": scatter_about(streams_of[0], (SEQUENCE_TOKENS, MODEL_WIDTH), 1.0, 6.0, ((0, 16),)),
        "queries": scatter_about(streams_of[1], (SEQUENCE_TOKENS, QUERY_HEADS * HEAD_SIZE), 1.0, 6.0, ((0, 16), (1, 2))),
        "key_matrix": scatter_about(streams_of[2], (MODEL_WIDTH, KEY_VALUE_HEADS * HEAD_SIZE), MODEL_WIDTH ** -0.5, 0.078125, ((0, 16), (1, 2))),
        "value_matrix": scatter_about(streams_of[3], (MODEL_WIDTH, KEY_VALUE_HEADS * HEAD_SIZE), MODEL_WIDTH ** -0.5, 0.078125, ((0, 16), (1, 2))),
        "readout": scatter_about(streams_of[4], (QUERY_HEADS * HEAD_SIZE, CAND), 1.0, 6.0, ((0, 2),)),
        "token_mask": plant((jax.random.randint(streams_of[5], (SEQUENCE_TOKENS,), 0, 5) < 1).astype(jnp.int32), jax.random.fold_in(streams_of[5], 1), 0, 1),
        "targets": plant(jax.random.randint(streams_of[6], (SEQUENCE_TOKENS,), 0, CAND), jax.random.fold_in(streams_of[6], 1), 0, CAND - 1).astype(jnp.int32),
    }


norm_eps = 1e-06
softcap = 30.0
score_scale = 168.0 ** (-0.5)

def normalized_rows(value_rows):
    inverse = lax.rsqrt(lax.optimization_barrier(jnp.mean(value_rows * value_rows, axis=-1, keepdims=True)) + norm_eps)
    return (value_rows * inverse, inverse)

def unit_norm_backward(unit, inverse, upstream):
    return inverse * (upstream - unit * lax.optimization_barrier(jnp.mean(unit * upstream, axis=-1, keepdims=True)))

def reference(inputs, queries, key_matrix, value_matrix, readout, token_mask, targets):
    query_groups = QUERY_HEADS // KEY_VALUE_HEADS
    span = WINDOW_KEYS + LOCAL_TOKENS
    blocks = SEQUENCE_TOKENS // LOCAL_TOKENS
    key_unscaled = jnp.dot(inputs, key_matrix, preferred_element_type=jnp.float32).reshape(SEQUENCE_TOKENS, KEY_VALUE_HEADS, HEAD_SIZE)
    value_rows = jnp.dot(inputs, value_matrix, preferred_element_type=jnp.float32).astype(jnp.bfloat16).reshape(SEQUENCE_TOKENS, KEY_VALUE_HEADS, HEAD_SIZE)
    key_unit_rows, key_inverse_norm = normalized_rows(key_unscaled)
    key_normalized_rows = key_unit_rows.astype(jnp.bfloat16)
    query_unit_rows, query_inverse_norm = normalized_rows(queries.astype(jnp.float32).reshape(SEQUENCE_TOKENS, KEY_VALUE_HEADS, query_groups, HEAD_SIZE))
    query_hat = query_unit_rows.astype(jnp.bfloat16)
    padded_keys = jnp.concatenate([jnp.zeros((WINDOW_KEYS, KEY_VALUE_HEADS, HEAD_SIZE), jnp.bfloat16), key_normalized_rows], axis=0)
    padded_values = jnp.concatenate([jnp.zeros((WINDOW_KEYS, KEY_VALUE_HEADS, HEAD_SIZE), jnp.bfloat16), value_rows], axis=0)
    readout_f = readout.astype(jnp.float32)

    def one_block(carry, index):
        key_running_sum, value_running_sum = carry
        start = (index * LOCAL_TOKENS).astype(jnp.int32)
        q_block = lax.dynamic_slice_in_dim(query_hat, start, LOCAL_TOKENS, 0).astype(jnp.float32)
        q_unit = lax.dynamic_slice_in_dim(query_unit_rows, start, LOCAL_TOKENS, 0)
        q_inverse = lax.dynamic_slice_in_dim(query_inverse_norm, start, LOCAL_TOKENS, 0)
        k_block = lax.dynamic_slice_in_dim(padded_keys, start, span, 0).astype(jnp.float32)
        v_block = lax.dynamic_slice_in_dim(padded_values, start, span, 0).astype(jnp.float32)
        chosen = lax.dynamic_slice_in_dim(token_mask, start, LOCAL_TOKENS, 0).astype(jnp.float32)[:, None]
        wanted = lax.dynamic_slice_in_dim(targets, start, LOCAL_TOKENS, 0)
        query_pos = start + jnp.arange(LOCAL_TOKENS, dtype=jnp.int32)
        key_pos = start - WINDOW_KEYS + jnp.arange(span, dtype=jnp.int32)
        distance = query_pos[:, None] - key_pos[None, :]
        visible = (distance >= 0) & (distance < WINDOW_KEYS) & (key_pos[None, :] >= 0)
        scores = jnp.einsum('qkgd,jkd->kgqj', q_block, k_block) * score_scale
        raised = jnp.where(visible, jnp.exp(scores), 0.0)
        attn = (raised / lax.optimization_barrier(jnp.sum(raised, axis=-1, keepdims=True))).astype(jnp.bfloat16)
        attn_f = attn.astype(jnp.float32)
        attended = jnp.einsum('kgqj,jkd->qkgd', attn_f, v_block).astype(jnp.bfloat16)
        flat = attended.reshape(LOCAL_TOKENS, QUERY_HEADS * HEAD_SIZE)
        logits = jnp.dot(flat, readout, preferred_element_type=jnp.float32)
        capped = softcap * jnp.tanh(logits / softcap)
        expo = jnp.exp(capped)
        probs = expo / lax.optimization_barrier(jnp.sum(expo, axis=-1, keepdims=True))
        onehot = (wanted[:, None] == jnp.arange(CAND, dtype=jnp.int32)[None, :]).astype(jnp.float32)
        dlogits = (chosen * (probs - onehot) * (1.0 - (capped / softcap) ** 2)).astype(jnp.bfloat16)
        attended_grad = jnp.dot(dlogits.astype(jnp.float32), readout_f.T).astype(jnp.bfloat16)
        attention_grad = attended_grad.astype(jnp.float32).reshape(LOCAL_TOKENS, KEY_VALUE_HEADS, query_groups, HEAD_SIZE)
        d_weights = jnp.einsum('qkgd,jkd->kgqj', attention_grad, v_block)
        d_scores = (attn_f * (d_weights - lax.optimization_barrier(jnp.sum(attn_f * d_weights, axis=-1, keepdims=True)))).astype(jnp.bfloat16).astype(jnp.float32)
        d_query_hat = jnp.einsum('kgqj,jkd->qkgd', d_scores, k_block) * score_scale
        d_key_hat = jnp.einsum('kgqj,qkgd->jkd', d_scores, q_block) * score_scale
        d_value = jnp.einsum('kgqj,qkgd->jkd', attn_f, attention_grad)
        q_grad = unit_norm_backward(q_unit, q_inverse, d_query_hat).reshape(LOCAL_TOKENS, QUERY_HEADS * HEAD_SIZE)
        key_running_sum = lax.dynamic_update_slice_in_dim(key_running_sum, lax.dynamic_slice_in_dim(key_running_sum, start, span, 0) + d_key_hat, start, 0)
        value_running_sum = lax.dynamic_update_slice_in_dim(value_running_sum, lax.dynamic_slice_in_dim(value_running_sum, start, span, 0) + d_value, start, 0)
        return ((key_running_sum, value_running_sum), q_grad)
    empty_running_sum = jnp.zeros((WINDOW_KEYS + SEQUENCE_TOKENS, KEY_VALUE_HEADS, HEAD_SIZE), jnp.float32)
    (key_running_sum, value_running_sum), q_grads = lax.scan(one_block, (empty_running_sum, empty_running_sum), jnp.arange(blocks, dtype=jnp.int32))
    query_grad = q_grads.reshape(SEQUENCE_TOKENS, QUERY_HEADS * HEAD_SIZE)
    key_weight_gradient = unit_norm_backward(key_unit_rows, key_inverse_norm, key_running_sum[WINDOW_KEYS:]).astype(jnp.bfloat16).reshape(SEQUENCE_TOKENS, KEY_VALUE_HEADS * HEAD_SIZE)
    value_weight_gradient = value_running_sum[WINDOW_KEYS:].astype(jnp.bfloat16).reshape(SEQUENCE_TOKENS, KEY_VALUE_HEADS * HEAD_SIZE)
    group_columns = KEY_VALUE_HEADS * HEAD_SIZE // N_HEAD
    input_grad = jnp.zeros((SEQUENCE_TOKENS, MODEL_WIDTH), jnp.float32)
    for group in range(N_HEAD):
        low = group * group_columns
        grads = jnp.concatenate([key_weight_gradient[:, low:low + group_columns], value_weight_gradient[:, low:low + group_columns]], axis=1)
        weights = jnp.concatenate([key_matrix[:, low:low + group_columns], value_matrix[:, low:low + group_columns]], axis=1)
        term = jnp.dot(grads, weights.T, preferred_element_type=jnp.float32).astype(jnp.bfloat16)
        input_grad = input_grad + term.astype(jnp.float32)
    return (query_grad, input_grad)
```

```python
import functools

import jax
import jax.numpy as jnp
from jax import lax
from jax.experimental import pallas as pl
from jax.experimental.pallas import tpu as pltpu
from jax.sharding import PartitionSpec as P

HEAD_SIZE = 128
WINDOW_KEYS = 1024
TILE = 256
GROUPS = 4

norm_eps = 1e-06
softcap = 30.0
score_scale = 168.0 ** (-0.5)
log2_scale = score_scale * 1.4426950408889634

VMEM_LIMIT = 48 * 1024 * 1024
NT = (((1,), (1,)), ((), ()))
TN = (((0,), (0,)), ((), ()))


def passed_along(value, axis, steps):
    count = lax.axis_size(axis)
    leading, last = (max(0, -steps), min(count, count - steps))
    return lax.ppermute(value, axis, [(source, source + steps) for source in range(leading, last)])


def swapped(value, axis):
    return lax.ppermute(value, axis, [(0, 1), (1, 0)])


def dot(a, b, dims=(((1,), (0,)), ((), ()))):
    return lax.dot_general(a, b, dims, preferred_element_type=jnp.float32)


def normalized_rows(value_rows):
    inverse = lax.rsqrt(jnp.mean(value_rows * value_rows, axis=-1, keepdims=True) + norm_eps)
    return (value_rows * inverse, inverse)


def unit_norm_backward(unit, inverse, upstream):
    return inverse * (upstream - unit * jnp.mean(unit * upstream, axis=-1, keepdims=True))


def prep_kernel(raw_ref, kv_ref):
    unit, _ = normalized_rows(raw_ref[:, :HEAD_SIZE])
    kv_ref[:, :HEAD_SIZE] = unit.astype(jnp.bfloat16)
    kv_ref[:, HEAD_SIZE:] = raw_ref[:, HEAD_SIZE:].astype(jnp.bfloat16)


def post_kernel(raw_ref, arrived_ref, own_ref, out_ref):
    unit, inverse = normalized_rows(raw_ref[:, :HEAD_SIZE])
    total = arrived_ref[...].astype(jnp.float32) + own_ref[...]
    out_ref[:, :HEAD_SIZE] = unit_norm_backward(unit, inverse, total[:, :HEAD_SIZE]).astype(
        jnp.bfloat16
    )
    out_ref[:, HEAD_SIZE:] = total[:, HEAD_SIZE:].astype(jnp.bfloat16)


def stacked_rows(ref, rows, group):
    parts = [ref[rows, g * HEAD_SIZE : (g + 1) * HEAD_SIZE] for g in range(group)]
    return jnp.concatenate(parts, axis=0)


def forward_kernel(reach, group, valid_ref, q_ref, *refs):
    kv_refs, (o_ref, sum_ref) = refs[: reach + 1], refs[reach + 1 :]
    tokens = q_ref.shape[0]
    spans = WINDOW_KEYS // TILE + 1
    rows = group * TILE
    for block in range(tokens // TILE):
        here = slice(block * TILE, (block + 1) * TILE)
        unit, _ = normalized_rows(stacked_rows(q_ref, here, group).astype(jnp.float32))
        q_hat = unit.astype(jnp.bfloat16)
        total = jnp.zeros((rows, 2 * HEAD_SIZE), jnp.float32)
        for c in range(spans):
            slot, low = divmod((block + c) * TILE, tokens)
            kv_ref = kv_refs[slot]
            key = kv_ref[low : low + TILE, :HEAD_SIZE]
            value = kv_ref[low : low + TILE, HEAD_SIZE:]
            raised = jnp.exp2(dot(q_hat, key, NT) * log2_scale)
            if c in (0, spans - 1):
                i = lax.broadcasted_iota(jnp.int32, (rows, TILE), 0) % TILE
                t = lax.broadcasted_iota(jnp.int32, (rows, TILE), 1)
                raised = jnp.where((t > i) if c == 0 else (t <= i), raised, 0.0)
            flag = jnp.full((TILE, HEAD_SIZE), valid_ref[slot], jnp.float32).astype(jnp.bfloat16)
            total += dot(raised.astype(jnp.bfloat16), jnp.concatenate([value, flag], axis=1))
        sums = total[:, HEAD_SIZE:]
        out = (total[:, :HEAD_SIZE] / sums).astype(jnp.bfloat16)
        for g in range(group):
            o_ref[here, g * HEAD_SIZE : (g + 1) * HEAD_SIZE] = out[g * TILE : (g + 1) * TILE]
        sum_ref[:, block * rows : (block + 1) * rows] = sums.T[:8]


def backward_kernel(reach, group, valid_ref, q_ref, o_ref, g_ref, sum_ref, *refs):
    kv_refs = refs[: reach + 1]
    qg_ref = refs[reach + 1]
    d_refs = refs[reach + 2 : 2 * reach + 3]
    acc_ref = refs[2 * reach + 3]
    tokens = q_ref.shape[0]
    spans = WINDOW_KEYS // TILE + 1
    rows = group * TILE
    acc_ref[...] = jnp.zeros_like(acc_ref)
    for block in range(tokens // TILE):
        here = slice(block * TILE, (block + 1) * TILE)
        unit, inverse = normalized_rows(stacked_rows(q_ref, here, group).astype(jnp.float32))
        q_hat = unit.astype(jnp.bfloat16)
        grad = stacked_rows(g_ref, here, group)
        out = stacked_rows(o_ref, here, group)
        product = grad.astype(jnp.float32) * out.astype(jnp.float32)
        delta = jnp.sum(product.T, axis=0, keepdims=True)
        inv = 1.0 / sum_ref[0:1, block * rows : (block + 1) * rows]
        dq = jnp.zeros((HEAD_SIZE, rows), jnp.float32)
        for c in range(spans):
            at = (block + c) * TILE
            slot, low = divmod(at, tokens)
            kv_ref = kv_refs[slot]
            key = kv_ref[low : low + TILE, :HEAD_SIZE]
            value = kv_ref[low : low + TILE, HEAD_SIZE:]
            raised = jnp.exp2(dot(key, q_hat, NT) * log2_scale)
            if c in (0, spans - 1):
                t = lax.broadcasted_iota(jnp.int32, (TILE, rows), 0)
                i = lax.broadcasted_iota(jnp.int32, (TILE, rows), 1) % TILE
                raised = jnp.where((t > i) if c == 0 else (t <= i), raised, 0.0)
            attn = raised * (inv * valid_ref[slot])
            attn16 = attn.astype(jnp.bfloat16)
            d_scores = (attn * (dot(value, grad, NT) - delta)).astype(jnp.bfloat16)
            acc_ref[at : at + TILE, :HEAD_SIZE] += dot(d_scores, q_hat)
            acc_ref[at : at + TILE, HEAD_SIZE:] += dot(attn16, grad)
            dq += dot(key, d_scores, TN)
        result = unit_norm_backward(unit, inverse, dq.T * score_scale)
        for g in range(group):
            qg_ref[here, g * HEAD_SIZE : (g + 1) * HEAD_SIZE] = result[g * TILE : (g + 1) * TILE]
    for slot in range(reach + 1):
        part = acc_ref[slot * tokens : (slot + 1) * tokens]
        d_refs[slot][:, :HEAD_SIZE] = (part[:, :HEAD_SIZE] * score_scale).astype(d_refs[slot].dtype)
        d_refs[slot][:, HEAD_SIZE:] = part[:, HEAD_SIZE:].astype(d_refs[slot].dtype)


def params():
    return pltpu.CompilerParams(vmem_limit_bytes=VMEM_LIMIT)


def columns(tokens, width, first=0):
    return pl.BlockSpec((tokens, width), lambda h: (0, first + h))


def prep(raw):
    tokens, width = raw.shape
    spec = columns(tokens, 2 * HEAD_SIZE)
    return pl.pallas_call(
        prep_kernel,
        grid=(width // (2 * HEAD_SIZE),),
        in_specs=[spec],
        out_specs=spec,
        out_shape=jax.ShapeDtypeStruct((tokens, width), jnp.bfloat16),
        compiler_params=params(),
        cost_estimate=pl.CostEstimate(
            flops=6 * tokens * width, bytes_accessed=6 * tokens * width, transcendentals=0
        ),
    )(raw)


def post(raw, arrived, own):
    tokens, width = raw.shape
    spec = columns(tokens, 2 * HEAD_SIZE)
    return pl.pallas_call(
        post_kernel,
        grid=(width // (2 * HEAD_SIZE),),
        in_specs=[spec] * 3,
        out_specs=spec,
        out_shape=jax.ShapeDtypeStruct((tokens, width), jnp.bfloat16),
        compiler_params=params(),
        cost_estimate=pl.CostEstimate(
            flops=12 * tokens * width, bytes_accessed=12 * tokens * width, transcendentals=0
        ),
    )(raw, arrived, own)


def attention_forward(valid, queries, window, first, heads, group):
    tokens = queries.shape[0]
    reach = len(window) - 1
    wide = group * HEAD_SIZE
    work = heads * group * tokens * (WINDOW_KEYS + TILE)
    return pl.pallas_call(
        functools.partial(forward_kernel, reach, group),
        grid=(heads,),
        in_specs=[pl.BlockSpec(memory_space=pltpu.SMEM), columns(tokens, wide, first)]
        + [columns(tokens, 2 * HEAD_SIZE)] * (reach + 1),
        out_specs=[
            columns(tokens, wide),
            pl.BlockSpec((8, group * tokens), lambda h: (h, 0)),
        ],
        out_shape=[
            jax.ShapeDtypeStruct((tokens, heads * wide), jnp.bfloat16),
            jax.ShapeDtypeStruct((heads * 8, group * tokens), jnp.float32),
        ],
        compiler_params=params(),
        cost_estimate=pl.CostEstimate(
            flops=8 * HEAD_SIZE * work, bytes_accessed=10 * tokens * heads * wide, transcendentals=work
        ),
    )(valid, queries, *window)


def attention_backward(valid, queries, attended, grad, sums, window, first, heads, group):
    tokens = queries.shape[0]
    reach = len(window) - 1
    wide = group * HEAD_SIZE
    work = heads * group * tokens * (WINDOW_KEYS + TILE)
    kinds = [jnp.bfloat16] + [jnp.float32] * reach
    return pl.pallas_call(
        functools.partial(backward_kernel, reach, group),
        grid=(heads,),
        in_specs=[
            pl.BlockSpec(memory_space=pltpu.SMEM),
            columns(tokens, wide, first),
            columns(tokens, wide),
            columns(tokens, wide, first),
            pl.BlockSpec((8, group * tokens), lambda h: (h, 0)),
        ]
        + [columns(tokens, 2 * HEAD_SIZE)] * (reach + 1),
        out_specs=[columns(tokens, wide)] + [columns(tokens, 2 * HEAD_SIZE)] * (reach + 1),
        out_shape=[jax.ShapeDtypeStruct((tokens, heads * wide), jnp.float32)]
        + [jax.ShapeDtypeStruct((tokens, heads * 2 * HEAD_SIZE), kind) for kind in kinds],
        scratch_shapes=[pltpu.VMEM(((reach + 1) * tokens, 2 * HEAD_SIZE), jnp.float32)],
        compiler_params=params(),
        cost_estimate=pl.CostEstimate(
            flops=16 * HEAD_SIZE * work, bytes_accessed=24 * tokens * heads * wide, transcendentals=work
        ),
    )(valid, queries, attended, grad, sums, *window)


def shards(inputs, queries, key_matrix, value_matrix, readout, token_mask, targets):
    tokens = inputs.shape[0]
    kv_width = key_matrix.shape[1]
    kv_heads = kv_width // HEAD_SIZE
    q_heads = queries.shape[1] // HEAD_SIZE
    group = q_heads // kv_heads
    reach = WINDOW_KEYS // tokens
    groups = min(GROUPS, kv_heads)
    heads = kv_heads // groups
    wide = heads * group * HEAD_SIZE
    position = lax.axis_index("seq")
    valid = (position >= reach - jnp.arange(reach + 1)).astype(jnp.float32)

    weights, raws, windows, outs, sums = [], [], [], [], []
    partial = None
    for n in range(groups):
        parts = []
        for h in range(n * heads, (n + 1) * heads):
            cols = slice(h * HEAD_SIZE, (h + 1) * HEAD_SIZE)
            parts += [key_matrix[:, cols], value_matrix[:, cols]]
        weight = lax.all_gather(jnp.concatenate(parts, axis=1), "seq", axis=0, tiled=True)
        raw = dot(inputs, weight)
        moving = prep(raw)
        window = [moving]
        for _ in range(reach):
            moving = passed_along(moving, "seq", 1)
            window.insert(0, moving)
        out, total = attention_forward(valid, queries, window, n * heads, heads, group)
        term = dot(out, readout[n * wide : (n + 1) * wide])
        partial = term if partial is None else partial + term
        weights.append(weight)
        raws.append(raw)
        windows.append(window)
        outs.append(out)
        sums.append(total)

    mine = partial.astype(jnp.bfloat16)
    if lax.axis_size("head") == 2:
        logits = mine.astype(jnp.float32) + swapped(mine, "head").astype(jnp.float32)
    else:
        logits = lax.psum(mine, "head").astype(jnp.float32)
    capped = softcap * jnp.tanh(logits / softcap)
    expo = jnp.exp(capped)
    probs = expo / jnp.sum(expo, axis=-1, keepdims=True)
    onehot = (targets[:, None] == jnp.arange(logits.shape[1], dtype=jnp.int32)[None, :]).astype(
        jnp.float32
    )
    chosen = token_mask.astype(jnp.float32)[:, None]
    dlogits = (chosen * (probs - onehot) * (1.0 - (capped / softcap) ** 2)).astype(jnp.bfloat16)
    attended_grad = dot(dlogits, readout, NT).astype(jnp.bfloat16)

    query_grads, grads = [], []
    for n in range(groups):
        query_grad, *pieces = attention_backward(
            valid, queries, outs[n], attended_grad, sums[n], windows[n], n * heads, heads, group
        )
        query_grads.append(query_grad)
        total = pieces[0]
        for slot in range(1, reach):
            arrived = passed_along(total, "seq", -1).astype(jnp.float32)
            total = (arrived + pieces[slot]).astype(jnp.bfloat16)
        grads.append(post(raws[n], passed_along(total, "seq", -1), pieces[reach]))

    def product(low, size):
        result = None
        for grad, weight in zip(grads, weights):
            term = dot(grad, lax.dynamic_slice_in_dim(weight, low, size, 0), NT)
            result = term if result is None else result + term
        return result.astype(jnp.bfloat16)

    model = weights[0].shape[0]
    if lax.axis_size("head") == 2:
        half = model // 2
        me = lax.axis_index("head")
        arrived = swapped(product((1 - me) * half, half), "head")
        input_grad = product(me * half, half).astype(jnp.float32) + arrived.astype(jnp.float32)
    else:
        input_grad = lax.psum_scatter(
            product(0, model), "head", scatter_dimension=1, tiled=True
        ).astype(jnp.float32)
    return (jnp.concatenate(query_grads, axis=1), input_grad)


def solution(mesh):
    in_specs = (
        P("seq", None),
        P("seq", "head"),
        P("seq", "head"),
        P("seq", "head"),
        P("head", None),
        P("seq"),
        P("seq"),
    )
    out_specs = (P("seq", "head"), P("seq", "head"))
    return jax.shard_map(shards, mesh=mesh, in_specs=in_specs, out_specs=out_specs, check_vma=False)
```

```python
import functools

import jax
import jax.numpy as jnp
from jax import lax
from jax.experimental import pallas as pl
from jax.experimental.pallas import tpu as pltpu
from jax.sharding import PartitionSpec as P

HEAD_SIZE = 128
WINDOW_KEYS = 1024
TILE = 256
GROUPS = 4
COLUMNS = 384

norm_eps = 1e-06
softcap = 30.0
score_scale = 168.0 ** (-0.5)
log2_scale = score_scale * 1.4426950408889634

VMEM_LIMIT = 48 * 1024 * 1024
NT = (((1,), (1,)), ((), ()))
TN = (((0,), (0,)), ((), ()))


def passed_along(value, axis, steps):
    count = lax.axis_size(axis)
    leading, last = (max(0, -steps), min(count, count - steps))
    return lax.ppermute(value, axis, [(source, source + steps) for source in range(leading, last)])


def swapped(value, axis):
    return lax.ppermute(value, axis, [(0, 1), (1, 0)])


def dot(a, b, dims=(((1,), (0,)), ((), ()))):
    return lax.dot_general(a, b, dims, preferred_element_type=jnp.float32)


def normalized_rows(value_rows):
    inverse = lax.rsqrt(jnp.mean(value_rows * value_rows, axis=-1, keepdims=True) + norm_eps)
    return (value_rows * inverse, inverse)


def unit_norm_backward(unit, inverse, upstream):
    return inverse * (upstream - unit * jnp.mean(unit * upstream, axis=-1, keepdims=True))


def project_kernel(x_ref, w_ref, raw_ref, kv_ref):
    raw_ref[...] = dot(x_ref[...], w_ref[...])
    unit, _ = normalized_rows(raw_ref[:, :HEAD_SIZE])
    kv_ref[:, :HEAD_SIZE] = unit.astype(jnp.bfloat16)
    kv_ref[:, HEAD_SIZE:] = raw_ref[:, HEAD_SIZE:].astype(jnp.bfloat16)


def product_kernel(count, start_ref, *refs):
    grads, weights, out_ref = refs[:count], refs[count : 2 * count], refs[2 * count]
    total = dot(grads[0][...], weights[0][...], NT)
    for n in range(1, count):
        total += dot(grads[n][...], weights[n][...], NT)
    out_ref[...] = total.astype(out_ref.dtype)


def post_kernel(raw_ref, arrived_ref, own_ref, out_ref):
    unit, inverse = normalized_rows(raw_ref[:, :HEAD_SIZE])
    total = arrived_ref[...].astype(jnp.float32) + own_ref[...]
    out_ref[:, :HEAD_SIZE] = unit_norm_backward(unit, inverse, total[:, :HEAD_SIZE]).astype(
        jnp.bfloat16
    )
    out_ref[:, HEAD_SIZE:] = total[:, HEAD_SIZE:].astype(jnp.bfloat16)


def stacked_rows(ref, rows, group):
    parts = [ref[rows, g * HEAD_SIZE : (g + 1) * HEAD_SIZE] for g in range(group)]
    return jnp.concatenate(parts, axis=0)


def forward_kernel(reach, group, valid_ref, q_ref, *refs):
    kv_refs, (o_ref, sum_ref) = refs[: reach + 1], refs[reach + 1 :]
    tokens = q_ref.shape[0]
    spans = WINDOW_KEYS // TILE + 1
    rows = group * TILE
    for block in range(tokens // TILE):
        here = slice(block * TILE, (block + 1) * TILE)
        unit, _ = normalized_rows(stacked_rows(q_ref, here, group).astype(jnp.float32))
        q_hat = unit.astype(jnp.bfloat16)
        total = jnp.zeros((rows, 2 * HEAD_SIZE), jnp.float32)
        for c in range(spans):
            slot, low = divmod((block + c) * TILE, tokens)
            kv_ref = kv_refs[slot]
            key = kv_ref[low : low + TILE, :HEAD_SIZE]
            value = kv_ref[low : low + TILE, HEAD_SIZE:]
            raised = jnp.exp2(dot(q_hat, key, NT) * log2_scale)
            if c in (0, spans - 1):
                i = lax.broadcasted_iota(jnp.int32, (rows, TILE), 0) % TILE
                t = lax.broadcasted_iota(jnp.int32, (rows, TILE), 1)
                raised = jnp.where((t > i) if c == 0 else (t <= i), raised, 0.0)
            flag = jnp.full((TILE, HEAD_SIZE), valid_ref[slot], jnp.float32).astype(jnp.bfloat16)
            total += dot(raised.astype(jnp.bfloat16), jnp.concatenate([value, flag], axis=1))
        sums = total[:, HEAD_SIZE:]
        out = (total[:, :HEAD_SIZE] / sums).astype(jnp.bfloat16)
        for g in range(group):
            o_ref[here, g * HEAD_SIZE : (g + 1) * HEAD_SIZE] = out[g * TILE : (g + 1) * TILE]
        sum_ref[:, block * rows : (block + 1) * rows] = sums.T[:8]


def backward_kernel(reach, group, valid_ref, q_ref, o_ref, g_ref, sum_ref, *refs):
    kv_refs = refs[: reach + 1]
    qg_ref = refs[reach + 1]
    d_refs = refs[reach + 2 : 2 * reach + 3]
    acc_ref = refs[2 * reach + 3]
    tokens = q_ref.shape[0]
    spans = WINDOW_KEYS // TILE + 1
    rows = group * TILE
    acc_ref[...] = jnp.zeros_like(acc_ref)
    for block in range(tokens // TILE):
        here = slice(block * TILE, (block + 1) * TILE)
        unit, inverse = normalized_rows(stacked_rows(q_ref, here, group).astype(jnp.float32))
        q_hat = unit.astype(jnp.bfloat16)
        grad = stacked_rows(g_ref, here, group)
        out = stacked_rows(o_ref, here, group)
        product = grad.astype(jnp.float32) * out.astype(jnp.float32)
        delta = jnp.sum(product.T, axis=0, keepdims=True)
        inv = 1.0 / sum_ref[0:1, block * rows : (block + 1) * rows]
        dq = jnp.zeros((HEAD_SIZE, rows), jnp.float32)
        for c in range(spans):
            at = (block + c) * TILE
            slot, low = divmod(at, tokens)
            kv_ref = kv_refs[slot]
            key = kv_ref[low : low + TILE, :HEAD_SIZE]
            value = kv_ref[low : low + TILE, HEAD_SIZE:]
            raised = jnp.exp2(dot(key, q_hat, NT) * log2_scale)
            if c in (0, spans - 1):
                t = lax.broadcasted_iota(jnp.int32, (TILE, rows), 0)
                i = lax.broadcasted_iota(jnp.int32, (TILE, rows), 1) % TILE
                raised = jnp.where((t > i) if c == 0 else (t <= i), raised, 0.0)
            attn = raised * (inv * valid_ref[slot])
            attn16 = attn.astype(jnp.bfloat16)
            d_scores = (attn * (dot(value, grad, NT) - delta)).astype(jnp.bfloat16)
            acc_ref[at : at + TILE, :HEAD_SIZE] += dot(d_scores, q_hat)
            acc_ref[at : at + TILE, HEAD_SIZE:] += dot(attn16, grad)
            dq += dot(key, d_scores, TN)
        result = unit_norm_backward(unit, inverse, dq.T * score_scale)
        for g in range(group):
            qg_ref[here, g * HEAD_SIZE : (g + 1) * HEAD_SIZE] = result[g * TILE : (g + 1) * TILE]
    for slot in range(reach + 1):
        part = acc_ref[slot * tokens : (slot + 1) * tokens]
        d_refs[slot][:, :HEAD_SIZE] = (part[:, :HEAD_SIZE] * score_scale).astype(d_refs[slot].dtype)
        d_refs[slot][:, HEAD_SIZE:] = part[:, HEAD_SIZE:].astype(d_refs[slot].dtype)


def params():
    return pltpu.CompilerParams(vmem_limit_bytes=VMEM_LIMIT)


def columns(tokens, width, first=0):
    return pl.BlockSpec((tokens, width), lambda h: (0, first + h))


def project(inputs, weight, first, heads):
    tokens, model = inputs.shape
    width = heads * 2 * HEAD_SIZE
    return pl.pallas_call(
        project_kernel,
        grid=(heads,),
        in_specs=[
            pl.BlockSpec((tokens, model), lambda h: (0, 0)),
            columns(model, 2 * HEAD_SIZE, first),
        ],
        out_specs=[columns(tokens, 2 * HEAD_SIZE)] * 2,
        out_shape=[
            jax.ShapeDtypeStruct((tokens, width), jnp.float32),
            jax.ShapeDtypeStruct((tokens, width), jnp.bfloat16),
        ],
        compiler_params=params(),
        cost_estimate=pl.CostEstimate(
            flops=2 * tokens * width * model,
            bytes_accessed=2 * model * (tokens + width) + 6 * tokens * width,
            transcendentals=0,
        ),
    )(inputs, weight)


def product(start, blocks, grads, weights):
    tokens, width = grads[0].shape
    count = len(grads)
    specs = [pl.BlockSpec((tokens, width), lambda i, s: (0, 0))] * count
    for _, at in weights:
        specs.append(pl.BlockSpec((COLUMNS, width), lambda i, s, at=at: (s[0] + i, at)))
    size = blocks * COLUMNS
    return pl.pallas_call(
        functools.partial(product_kernel, count),
        grid_spec=pltpu.PrefetchScalarGridSpec(
            num_scalar_prefetch=1,
            grid=(blocks,),
            in_specs=specs,
            out_specs=pl.BlockSpec((tokens, COLUMNS), lambda i, s: (0, i)),
        ),
        out_shape=jax.ShapeDtypeStruct((tokens, size), jnp.bfloat16),
        compiler_params=params(),
        cost_estimate=pl.CostEstimate(
            flops=2 * tokens * width * count * size,
            bytes_accessed=2 * width * count * (tokens + size) + 2 * tokens * size,
            transcendentals=0,
        ),
    )(jnp.reshape(start, (1,)).astype(jnp.int32), *grads, *[array for array, _ in weights])


def post(raw, arrived, own):
    tokens, width = raw.shape
    spec = columns(tokens, 2 * HEAD_SIZE)
    return pl.pallas_call(
        post_kernel,
        grid=(width // (2 * HEAD_SIZE),),
        in_specs=[spec] * 3,
        out_specs=spec,
        out_shape=jax.ShapeDtypeStruct((tokens, width), jnp.bfloat16),
        compiler_params=params(),
        cost_estimate=pl.CostEstimate(
            flops=12 * tokens * width, bytes_accessed=12 * tokens * width, transcendentals=0
        ),
    )(raw, arrived, own)


def attention_forward(valid, queries, window, first, heads, group):
    tokens = queries.shape[0]
    reach = len(window) - 1
    wide = group * HEAD_SIZE
    work = heads * group * tokens * (WINDOW_KEYS + TILE)
    return pl.pallas_call(
        functools.partial(forward_kernel, reach, group),
        grid=(heads,),
        in_specs=[pl.BlockSpec(memory_space=pltpu.SMEM), columns(tokens, wide, first)]
        + [columns(tokens, 2 * HEAD_SIZE)] * (reach + 1),
        out_specs=[
            columns(tokens, wide),
            pl.BlockSpec((8, group * tokens), lambda h: (h, 0)),
        ],
        out_shape=[
            jax.ShapeDtypeStruct((tokens, heads * wide), jnp.bfloat16),
            jax.ShapeDtypeStruct((heads * 8, group * tokens), jnp.float32),
        ],
        compiler_params=params(),
        cost_estimate=pl.CostEstimate(
            flops=8 * HEAD_SIZE * work, bytes_accessed=10 * tokens * heads * wide, transcendentals=work
        ),
    )(valid, queries, *window)


def attention_backward(valid, queries, attended, grad, sums, window, first, heads, group):
    tokens = queries.shape[0]
    reach = len(window) - 1
    wide = group * HEAD_SIZE
    work = heads * group * tokens * (WINDOW_KEYS + TILE)
    kinds = [jnp.bfloat16] + [jnp.float32] * reach
    return pl.pallas_call(
        functools.partial(backward_kernel, reach, group),
        grid=(heads,),
        in_specs=[
            pl.BlockSpec(memory_space=pltpu.SMEM),
            columns(tokens, wide, first),
            columns(tokens, wide),
            columns(tokens, wide, first),
            pl.BlockSpec((8, group * tokens), lambda h: (h, 0)),
        ]
        + [columns(tokens, 2 * HEAD_SIZE)] * (reach + 1),
        out_specs=[columns(tokens, wide)] + [columns(tokens, 2 * HEAD_SIZE)] * (reach + 1),
        out_shape=[jax.ShapeDtypeStruct((tokens, heads * wide), jnp.float32)]
        + [jax.ShapeDtypeStruct((tokens, heads * 2 * HEAD_SIZE), kind) for kind in kinds],
        scratch_shapes=[pltpu.VMEM(((reach + 1) * tokens, 2 * HEAD_SIZE), jnp.float32)],
        compiler_params=params(),
        cost_estimate=pl.CostEstimate(
            flops=16 * HEAD_SIZE * work, bytes_accessed=24 * tokens * heads * wide, transcendentals=work
        ),
    )(valid, queries, attended, grad, sums, *window)


def shards(inputs, queries, key_matrix, value_matrix, readout, token_mask, targets):
    tokens = inputs.shape[0]
    kv_width = key_matrix.shape[1]
    kv_heads = kv_width // HEAD_SIZE
    q_heads = queries.shape[1] // HEAD_SIZE
    group = q_heads // kv_heads
    reach = WINDOW_KEYS // tokens
    groups = min(GROUPS, kv_heads)
    heads = kv_heads // groups
    wide = heads * group * HEAD_SIZE
    position = lax.axis_index("seq")
    valid = (position >= reach - jnp.arange(reach + 1)).astype(jnp.float32)

    parts = []
    for h in range(kv_heads):
        cols = slice(h * HEAD_SIZE, (h + 1) * HEAD_SIZE)
        parts += [key_matrix[:, cols], value_matrix[:, cols]]
    weight = lax.all_gather(jnp.concatenate(parts, axis=1), "seq", axis=0, tiled=True)

    raws, windows, outs, sums = [], [], [], []
    partial = None
    for n in range(groups):
        raw, moving = project(inputs, weight, n * heads, heads)
        window = [moving]
        for _ in range(reach):
            moving = passed_along(moving, "seq", 1)
            window.insert(0, moving)
        out, total = attention_forward(valid, queries, window, n * heads, heads, group)
        term = dot(out, readout[n * wide : (n + 1) * wide])
        partial = term if partial is None else partial + term
        raws.append(raw)
        windows.append(window)
        outs.append(out)
        sums.append(total)

    mine = partial.astype(jnp.bfloat16)
    if lax.axis_size("head") == 2:
        logits = mine.astype(jnp.float32) + swapped(mine, "head").astype(jnp.float32)
    else:
        logits = lax.psum(mine, "head").astype(jnp.float32)
    capped = softcap * jnp.tanh(logits / softcap)
    expo = jnp.exp(capped)
    probs = expo / jnp.sum(expo, axis=-1, keepdims=True)
    onehot = (targets[:, None] == jnp.arange(logits.shape[1], dtype=jnp.int32)[None, :]).astype(
        jnp.float32
    )
    chosen = token_mask.astype(jnp.float32)[:, None]
    dlogits = (chosen * (probs - onehot) * (1.0 - (capped / softcap) ** 2)).astype(jnp.bfloat16)
    attended_grad = dot(dlogits, readout, NT).astype(jnp.bfloat16)

    query_grads, grads = [], []
    for n in range(groups):
        query_grad, *pieces = attention_backward(
            valid, queries, outs[n], attended_grad, sums[n], windows[n], n * heads, heads, group
        )
        query_grads.append(query_grad)
        total = pieces[0]
        for slot in range(1, reach):
            arrived = passed_along(total, "seq", -1).astype(jnp.float32)
            total = (arrived + pieces[slot]).astype(jnp.bfloat16)
        grads.append(post(raws[n], passed_along(total, "seq", -1), pieces[reach]))

    blocks = weight.shape[0] // COLUMNS
    factors = [(weight, n) for n in range(groups)]
    if lax.axis_size("head") == 2:
        half = blocks // 2
        me = lax.axis_index("head")
        arrived = []
        done = 0
        for size in (half // 3, half // 3, half - 2 * (half // 3)):
            term = product((1 - me) * half + done, size, grads, factors)
            arrived.append(swapped(term, "head"))
            done += size
        own = product(me * half, half, grads, factors)
        input_grad = own.astype(jnp.float32) + jnp.concatenate(arrived, axis=1).astype(jnp.float32)
    else:
        input_grad = lax.psum_scatter(
            product(0, blocks, grads, factors), "head", scatter_dimension=1, tiled=True
        ).astype(jnp.float32)
    return (jnp.concatenate(query_grads, axis=1), input_grad)


def solution(mesh):
    in_specs = (
        P("seq", None),
        P("seq", "head"),
        P("seq", "head"),
        P("seq", "head"),
        P("head", None),
        P("seq"),
        P("seq"),
    )
    out_specs = (P("seq", "head"), P("seq", "head"))
    return jax.shard_map(shards, mesh=mesh, in_specs=in_specs, out_specs=out_specs, check_vma=False)
```

```python
import functools

import jax
import jax.numpy as jnp
from jax import lax
from jax.experimental import pallas as pl
from jax.experimental.pallas import tpu as pltpu
from jax.sharding import PartitionSpec as P

HEAD_SIZE = 128
WINDOW_KEYS = 1024
TILE = 256
FORWARD_GROUPS = 2
BACKWARD_GROUPS = 4
COLUMNS = 384

norm_eps = 1e-06
softcap = 30.0
score_scale = 168.0 ** (-0.5)
log2_scale = score_scale * 1.4426950408889634

VMEM_LIMIT = 48 * 1024 * 1024
NT = (((1,), (1,)), ((), ()))
TN = (((0,), (0,)), ((), ()))


def passed_along(value, axis, steps):
    count = lax.axis_size(axis)
    leading, last = (max(0, -steps), min(count, count - steps))
    return lax.ppermute(value, axis, [(source, source + steps) for source in range(leading, last)])


def swapped(value, axis):
    return lax.ppermute(value, axis, [(0, 1), (1, 0)])


def dot(a, b, dims=(((1,), (0,)), ((), ()))):
    return lax.dot_general(a, b, dims, preferred_element_type=jnp.float32)


def normalized_rows(value_rows):
    inverse = lax.rsqrt(jnp.mean(value_rows * value_rows, axis=-1, keepdims=True) + norm_eps)
    return (value_rows * inverse, inverse)


def unit_norm_backward(unit, inverse, upstream):
    return inverse * (upstream - unit * jnp.mean(unit * upstream, axis=-1, keepdims=True))


def project_kernel(x_ref, w_ref, raw_ref, kv_ref):
    raw_ref[...] = dot(x_ref[...], w_ref[...])
    unit, _ = normalized_rows(raw_ref[:, :HEAD_SIZE])
    kv_ref[:, :HEAD_SIZE] = unit.astype(jnp.bfloat16)
    kv_ref[:, HEAD_SIZE:] = raw_ref[:, HEAD_SIZE:].astype(jnp.bfloat16)


def interleave_kernel(k_ref, v_ref, out_ref):
    for h in range(k_ref.shape[1] // HEAD_SIZE):
        cols = slice(h * HEAD_SIZE, (h + 1) * HEAD_SIZE)
        low = 2 * h * HEAD_SIZE
        out_ref[:, low : low + HEAD_SIZE] = k_ref[:, cols]
        out_ref[:, low + HEAD_SIZE : low + 2 * HEAD_SIZE] = v_ref[:, cols]


def product_kernel(count, start_ref, *refs):
    grads, weights, out_ref = refs[:count], refs[count : 2 * count], refs[2 * count]
    total = dot(grads[0][...], weights[0][...], NT)
    for n in range(1, count):
        total += dot(grads[n][...], weights[n][...], NT)
    out_ref[...] = total.astype(out_ref.dtype)


def post_kernel(raw_ref, arrived_ref, own_ref, out_ref):
    unit, inverse = normalized_rows(raw_ref[:, :HEAD_SIZE])
    total = arrived_ref[...].astype(jnp.float32) + own_ref[...]
    out_ref[:, :HEAD_SIZE] = unit_norm_backward(unit, inverse, total[:, :HEAD_SIZE]).astype(
        jnp.bfloat16
    )
    out_ref[:, HEAD_SIZE:] = total[:, HEAD_SIZE:].astype(jnp.bfloat16)


def stacked_rows(ref, rows, group):
    parts = [ref[rows, g * HEAD_SIZE : (g + 1) * HEAD_SIZE] for g in range(group)]
    return jnp.concatenate(parts, axis=0)


def forward_kernel(reach, group, valid_ref, q_ref, *refs):
    kv_refs, (o_ref, sum_ref) = refs[: reach + 1], refs[reach + 1 :]
    tokens = q_ref.shape[0]
    spans = WINDOW_KEYS // TILE + 1
    rows = group * TILE
    for block in range(tokens // TILE):
        here = slice(block * TILE, (block + 1) * TILE)
        unit, _ = normalized_rows(stacked_rows(q_ref, here, group).astype(jnp.float32))
        q_hat = unit.astype(jnp.bfloat16)
        total = jnp.zeros((rows, 2 * HEAD_SIZE), jnp.float32)
        for c in range(spans):
            slot, low = divmod((block + c) * TILE, tokens)
            kv_ref = kv_refs[slot]
            key = kv_ref[low : low + TILE, :HEAD_SIZE]
            value = kv_ref[low : low + TILE, HEAD_SIZE:]
            raised = jnp.exp2(dot(q_hat, key, NT) * log2_scale)
            if c in (0, spans - 1):
                i = lax.broadcasted_iota(jnp.int32, (rows, TILE), 0) % TILE
                t = lax.broadcasted_iota(jnp.int32, (rows, TILE), 1)
                raised = jnp.where((t > i) if c == 0 else (t <= i), raised, 0.0)
            flag = jnp.full((TILE, HEAD_SIZE), valid_ref[slot], jnp.float32).astype(jnp.bfloat16)
            total += dot(raised.astype(jnp.bfloat16), jnp.concatenate([value, flag], axis=1))
        sums = total[:, HEAD_SIZE:]
        out = (total[:, :HEAD_SIZE] / sums).astype(jnp.bfloat16)
        for g in range(group):
            o_ref[here, g * HEAD_SIZE : (g + 1) * HEAD_SIZE] = out[g * TILE : (g + 1) * TILE]
        sum_ref[:, block * rows : (block + 1) * rows] = sums.T[:8]


def backward_kernel(reach, group, valid_ref, q_ref, o_ref, g_ref, sum_ref, *refs):
    kv_refs = refs[: reach + 1]
    qg_ref = refs[reach + 1]
    d_refs = refs[reach + 2 : 2 * reach + 3]
    acc_ref = refs[2 * reach + 3]
    tokens = q_ref.shape[0]
    spans = WINDOW_KEYS // TILE + 1
    rows = group * TILE
    acc_ref[...] = jnp.zeros_like(acc_ref)
    for block in range(tokens // TILE):
        here = slice(block * TILE, (block + 1) * TILE)
        unit, inverse = normalized_rows(stacked_rows(q_ref, here, group).astype(jnp.float32))
        q_hat = unit.astype(jnp.bfloat16)
        grad = stacked_rows(g_ref, here, group)
        out = stacked_rows(o_ref, here, group)
        product = grad.astype(jnp.float32) * out.astype(jnp.float32)
        delta = jnp.sum(product.T, axis=0, keepdims=True)
        inv = 1.0 / sum_ref[0:1, block * rows : (block + 1) * rows]
        dq = jnp.zeros((HEAD_SIZE, rows), jnp.float32)
        for c in range(spans):
            at = (block + c) * TILE
            slot, low = divmod(at, tokens)
            kv_ref = kv_refs[slot]
            key = kv_ref[low : low + TILE, :HEAD_SIZE]
            value = kv_ref[low : low + TILE, HEAD_SIZE:]
            raised = jnp.exp2(dot(key, q_hat, NT) * log2_scale)
            if c in (0, spans - 1):
                t = lax.broadcasted_iota(jnp.int32, (TILE, rows), 0)
                i = lax.broadcasted_iota(jnp.int32, (TILE, rows), 1) % TILE
                raised = jnp.where((t > i) if c == 0 else (t <= i), raised, 0.0)
            attn = raised * (inv * valid_ref[slot])
            attn16 = attn.astype(jnp.bfloat16)
            d_scores = (attn * (dot(value, grad, NT) - delta)).astype(jnp.bfloat16)
            acc_ref[at : at + TILE, :HEAD_SIZE] += dot(d_scores, q_hat)
            acc_ref[at : at + TILE, HEAD_SIZE:] += dot(attn16, grad)
            dq += dot(key, d_scores, TN)
        result = unit_norm_backward(unit, inverse, dq.T * score_scale)
        for g in range(group):
            qg_ref[here, g * HEAD_SIZE : (g + 1) * HEAD_SIZE] = result[g * TILE : (g + 1) * TILE]
    for slot in range(reach + 1):
        part = acc_ref[slot * tokens : (slot + 1) * tokens]
        d_refs[slot][:, :HEAD_SIZE] = (part[:, :HEAD_SIZE] * score_scale).astype(d_refs[slot].dtype)
        d_refs[slot][:, HEAD_SIZE:] = part[:, HEAD_SIZE:].astype(d_refs[slot].dtype)


def params():
    return pltpu.CompilerParams(vmem_limit_bytes=VMEM_LIMIT)


def columns(tokens, width, first=0):
    return pl.BlockSpec((tokens, width), lambda h: (0, first + h))


def interleave(keys, values):
    rows, width = keys.shape
    return pl.pallas_call(
        interleave_kernel,
        out_shape=jax.ShapeDtypeStruct((rows, 2 * width), keys.dtype),
        compiler_params=params(),
    )(keys, values)


def project(inputs, weight, first, heads):
    tokens, model = inputs.shape
    width = heads * 2 * HEAD_SIZE
    return pl.pallas_call(
        project_kernel,
        grid=(heads,),
        in_specs=[
            pl.BlockSpec((tokens, model), lambda h: (0, 0)),
            columns(model, 2 * HEAD_SIZE, first),
        ],
        out_specs=[columns(tokens, 2 * HEAD_SIZE)] * 2,
        out_shape=[
            jax.ShapeDtypeStruct((tokens, width), jnp.float32),
            jax.ShapeDtypeStruct((tokens, width), jnp.bfloat16),
        ],
        compiler_params=params(),
        cost_estimate=pl.CostEstimate(
            flops=2 * tokens * width * model,
            bytes_accessed=2 * model * (tokens + width) + 6 * tokens * width,
            transcendentals=0,
        ),
    )(inputs, weight)


def product(start, blocks, grads, weights):
    tokens, width = grads[0].shape
    count = len(grads)
    specs = [pl.BlockSpec((tokens, width), lambda i, s: (0, 0))] * count
    for _, at in weights:
        specs.append(pl.BlockSpec((COLUMNS, width), lambda i, s, at=at: (s[0] + i, at)))
    size = blocks * COLUMNS
    return pl.pallas_call(
        functools.partial(product_kernel, count),
        grid_spec=pltpu.PrefetchScalarGridSpec(
            num_scalar_prefetch=1,
            grid=(blocks,),
            in_specs=specs,
            out_specs=pl.BlockSpec((tokens, COLUMNS), lambda i, s: (0, i)),
        ),
        out_shape=jax.ShapeDtypeStruct((tokens, size), jnp.bfloat16),
        compiler_params=params(),
        cost_estimate=pl.CostEstimate(
            flops=2 * tokens * width * count * size,
            bytes_accessed=2 * width * count * (tokens + size) + 2 * tokens * size,
            transcendentals=0,
        ),
    )(jnp.reshape(start, (1,)).astype(jnp.int32), *grads, *[array for array, _ in weights])


def post(raw, arrived, own, first):
    tokens, width = own.shape
    spec = columns(tokens, 2 * HEAD_SIZE)
    return pl.pallas_call(
        post_kernel,
        grid=(width // (2 * HEAD_SIZE),),
        in_specs=[columns(tokens, 2 * HEAD_SIZE, first), spec, spec],
        out_specs=spec,
        out_shape=jax.ShapeDtypeStruct((tokens, width), jnp.bfloat16),
        compiler_params=params(),
        cost_estimate=pl.CostEstimate(
            flops=12 * tokens * width, bytes_accessed=12 * tokens * width, transcendentals=0
        ),
    )(raw, arrived, own)


def attention_forward(valid, queries, window, first, heads, group):
    tokens = queries.shape[0]
    reach = len(window) - 1
    wide = group * HEAD_SIZE
    work = heads * group * tokens * (WINDOW_KEYS + TILE)
    return pl.pallas_call(
        functools.partial(forward_kernel, reach, group),
        grid=(heads,),
        in_specs=[pl.BlockSpec(memory_space=pltpu.SMEM), columns(tokens, wide, first)]
        + [columns(tokens, 2 * HEAD_SIZE)] * (reach + 1),
        out_specs=[
            columns(tokens, wide),
            pl.BlockSpec((8, group * tokens), lambda h: (h, 0)),
        ],
        out_shape=[
            jax.ShapeDtypeStruct((tokens, heads * wide), jnp.bfloat16),
            jax.ShapeDtypeStruct((heads * 8, group * tokens), jnp.float32),
        ],
        compiler_params=params(),
        cost_estimate=pl.CostEstimate(
            flops=8 * HEAD_SIZE * work, bytes_accessed=10 * tokens * heads * wide, transcendentals=work
        ),
    )(valid, queries, *window)


def attention_backward(valid, queries, attended, grad, sums, window, first, inner, heads, group):
    tokens = queries.shape[0]
    reach = len(window) - 1
    wide = group * HEAD_SIZE
    work = heads * group * tokens * (WINDOW_KEYS + TILE)
    kinds = [jnp.bfloat16] + [jnp.float32] * reach
    return pl.pallas_call(
        functools.partial(backward_kernel, reach, group),
        grid=(heads,),
        in_specs=[
            pl.BlockSpec(memory_space=pltpu.SMEM),
            columns(tokens, wide, first),
            columns(tokens, wide, inner),
            columns(tokens, wide, first),
            pl.BlockSpec((8, group * tokens), lambda h: (inner + h, 0)),
        ]
        + [columns(tokens, 2 * HEAD_SIZE, inner)] * (reach + 1),
        out_specs=[columns(tokens, wide)] + [columns(tokens, 2 * HEAD_SIZE)] * (reach + 1),
        out_shape=[jax.ShapeDtypeStruct((tokens, heads * wide), jnp.float32)]
        + [jax.ShapeDtypeStruct((tokens, heads * 2 * HEAD_SIZE), kind) for kind in kinds],
        scratch_shapes=[pltpu.VMEM(((reach + 1) * tokens, 2 * HEAD_SIZE), jnp.float32)],
        compiler_params=params(),
        cost_estimate=pl.CostEstimate(
            flops=16 * HEAD_SIZE * work, bytes_accessed=24 * tokens * heads * wide, transcendentals=work
        ),
    )(valid, queries, attended, grad, sums, *window)


def shards(inputs, queries, key_matrix, value_matrix, readout, token_mask, targets):
    tokens = inputs.shape[0]
    kv_width = key_matrix.shape[1]
    kv_heads = kv_width // HEAD_SIZE
    q_heads = queries.shape[1] // HEAD_SIZE
    group = q_heads // kv_heads
    reach = WINDOW_KEYS // tokens
    groups = min(FORWARD_GROUPS, kv_heads)
    heads = kv_heads // groups
    wide = heads * group * HEAD_SIZE
    position = lax.axis_index("seq")
    valid = (position >= reach - jnp.arange(reach + 1)).astype(jnp.float32)

    weight = lax.all_gather(interleave(key_matrix, value_matrix), "seq", axis=0, tiled=True)

    raws, windows, outs, sums = [], [], [], []
    partial = None
    for n in range(groups):
        raw, moving = project(inputs, weight, n * heads, heads)
        window = [moving]
        for _ in range(reach):
            moving = passed_along(moving, "seq", 1)
            window.insert(0, moving)
        out, total = attention_forward(valid, queries, window, n * heads, heads, group)
        term = dot(out, readout[n * wide : (n + 1) * wide])
        partial = term if partial is None else partial + term
        raws.append(raw)
        windows.append(window)
        outs.append(out)
        sums.append(total)

    mine = partial.astype(jnp.bfloat16)
    if lax.axis_size("head") == 2:
        logits = mine.astype(jnp.float32) + swapped(mine, "head").astype(jnp.float32)
    else:
        logits = lax.psum(mine, "head").astype(jnp.float32)
    capped = softcap * jnp.tanh(logits / softcap)
    expo = jnp.exp(capped)
    probs = expo / jnp.sum(expo, axis=-1, keepdims=True)
    onehot = (targets[:, None] == jnp.arange(logits.shape[1], dtype=jnp.int32)[None, :]).astype(
        jnp.float32
    )
    chosen = token_mask.astype(jnp.float32)[:, None]
    dlogits = (chosen * (probs - onehot) * (1.0 - (capped / softcap) ** 2)).astype(jnp.bfloat16)
    attended_grad = dot(dlogits, readout, NT).astype(jnp.bfloat16)

    query_grads, grads, pending = [], [], []
    parts = min(BACKWARD_GROUPS, kv_heads)
    some = kv_heads // parts
    for n in range(parts):
        if n >= 2:
            attended_grad, pending[n - 2] = lax.optimization_barrier(
                (attended_grad, pending[n - 2])
            )
        if n >= 3:
            grads[n - 3] = post(*grads[n - 3])
            attended_grad, grads[n - 3] = lax.optimization_barrier((attended_grad, grads[n - 3]))
        at, inner = divmod(n * some, heads)
        query_grad, *pieces = attention_backward(
            valid, queries, outs[at], attended_grad, sums[at], windows[at], n * some, inner, some, group
        )
        query_grads.append(query_grad)
        total = pieces[0]
        for slot in range(1, reach):
            arrived = passed_along(total, "seq", -1).astype(jnp.float32)
            total = (arrived + pieces[slot]).astype(jnp.bfloat16)
        pending.append(total)
        grads.append((raws[at], passed_along(total, "seq", -1), pieces[reach], inner))
    grads = [post(*item) if isinstance(item, tuple) else item for item in grads]

    blocks = weight.shape[0] // COLUMNS
    factors = [(weight, n) for n in range(parts)]
    if lax.axis_size("head") == 2:
        half = blocks // 2
        me = lax.axis_index("head")
        arrived = []
        done = 0
        rest = (half - 1) // 2
        for size in (1, rest, half - 1 - rest):
            term = product((1 - me) * half + done, size, grads, factors)
            arrived.append(swapped(term, "head"))
            done += size
        own = product(me * half, half, grads, factors)
        input_grad = own.astype(jnp.float32) + jnp.concatenate(arrived, axis=1).astype(jnp.float32)
    else:
        input_grad = lax.psum_scatter(
            product(0, blocks, grads, factors), "head", scatter_dimension=1, tiled=True
        ).astype(jnp.float32)
    return (jnp.concatenate(query_grads, axis=1), input_grad)


def solution(mesh):
    in_specs = (
        P("seq", None),
        P("seq", "head"),
        P("seq", "head"),
        P("seq", "head"),
        P("head", None),
        P("seq"),
        P("seq"),
    )
    out_specs = (P("seq", "head"), P("seq", "head"))
    return jax.shard_map(shards, mesh=mesh, in_specs=in_specs, out_specs=out_specs, check_vma=False)
```
